32 devices in a mesh: dp: 8 (over z, x), expert: 4 (over y, core).
Axes of the slice: x: 2, y: 2, z: 4, core: 2. Of those that a mesh axis runs over, the one named last changes fastest.
Arguments:
- tokens: bfloat16 [1024, 4096], P('dp'), may hold values from -6 to 6
- w_gate: bfloat16 [4, 4096, 8192], P('expert', None, 'dp'), may hold values from -0.09375 to 0.09375
- w_up: bfloat16 [4, 4096, 8192], P('expert', None, 'dp'), may hold values from -0.09375 to 0.09375
- w_down: bfloat16 [4, 8192, 4096], P('expert', 'dp'), may hold values from -0.0625 to 0.0625
- chosen: int32 [4, 8, 2], P(None, 'dp'), may hold values from 0 to 127, as said below
- counts: int32 [4, 8], P(None, 'dp'), may hold values from 0 to 2, as said below
- gate_codes: int32 [4, 8, 2], P(None, 'dp'), may hold values from 16384 to 65536
Outputs:
- combined: bfloat16 [1024, 4096], P('dp', 'expert')
The draws below stay inside these ranges and needn't reach their ends.
Inputs may be any that keep to these rules, and one draw needn't show every extreme that they name: `chosen`: the 2 entries of one expert's block for one shard are distinct. `counts`: one expert has all 2 slots live in every token shard.
All inputs are finite; a program needn't handle non-finite values.
Results may differ from the reference program's by a relative error of at most 0.005.
Values may be sent and summed in bfloat16 or wider, within the bound.
A program may use at most 64 MiB of HBM per device.

```python
import jax
import jax.numpy as jnp
from jax import lax

D = 4096
FF = 8192
TOK_DEV = 128
SLOTS = 2
EXPERTS = 4
TOKENS = 1024
N_DP = 8


def draw_chosen(key, part):
    key = jax.random.fold_in(key, 11)
    first_key, step_key = jax.random.split(key)
    first = jax.random.randint(first_key, (EXPERTS, N_DP, 1), 0, TOK_DEV).astype(jnp.int32)
    steps = jax.random.randint(step_key, (EXPERTS, N_DP, SLOTS - 1), 1, TOK_DEV // SLOTS + 1).astype(jnp.int32)
    offsets = jnp.concatenate([jnp.zeros((EXPERTS, N_DP, 1), jnp.int32), jnp.cumsum(steps, axis=2).astype(jnp.int32)], axis=2)
    return ((first + offsets) % TOK_DEV).astype(jnp.int32)


def draw_counts(key, part):
    key = jax.random.fold_in(key, 23)
    base_key, hot_key, full_key = jax.random.split(key, 3)
    base = jax.random.randint(base_key, (EXPERTS, N_DP), 0, SLOTS).astype(jnp.int32)
    hot_shard = jax.random.randint(hot_key, (1, N_DP), 0, 4) == 0
    full_expert = jax.random.randint(full_key, (), 0, EXPERTS)
    expert_ids = jnp.arange(EXPERTS, dtype=jnp.int32)[:, None]
    filled = jnp.logical_or(hot_shard, expert_ids == full_expert)
    return jnp.where(filled, SLOTS, base).astype(jnp.int32)


def with_ends(entries, own_key, smallest, largest):
    shape = entries.shape
    spot = [jax.random.randint(jax.random.fold_in(own_key, axis), (), 0, shape[axis]) for axis in range(len(shape))]
    entries = entries.at[tuple(spot)].set(smallest)
    longest = shape.index(max(shape))
    spot[longest] = (spot[longest] + 1) % shape[longest]
    return entries.at[tuple(spot)].set(largest)


def shard_levels(own_key, shape, cuts, low, largest):
    level, own = 1.0, jax.random.fold_in(own_key, 6)
    for dim, parts in cuts:
        heights = jnp.exp(jax.random.uniform(jax.random.fold_in(own, dim), (parts,), jnp.float32, low / len(cuts), largest / len(cuts)))
        level = level * jnp.repeat(heights, shape[dim] // parts).reshape([-1 if axis == dim else 1 for axis in range(len(shape))])
    return level


def bell_draw(stream_key, dims, width, most, pieces=(), kind=jnp.bfloat16):
    values = width * jax.random.normal(stream_key, dims, jnp.float32)
    if pieces:
        values = values * shard_levels(stream_key, dims, pieces, -0.22, 0.18)
    return jnp.clip(values, -most, most).astype(kind)


def setup_inputs(seed: int = 0) -> dict:
    seeds = jax.random.split(jax.random.key(seed), 8)
    tokens = bell_draw(seeds[0], (TOKENS, D), 1.0, 6.0, ((0, 8),))
    w_gate = bell_draw(seeds[1], (EXPERTS, D, FF), D ** -0.5, 0.09375, ((0, 4), (2, 8)))
    w_up = bell_draw(seeds[2], (EXPERTS, D, FF), D ** -0.5, 0.09375, ((0, 4), (2, 8)))
    w_down = bell_draw(seeds[3], (EXPERTS, FF, D), FF ** -0.5, 0.0625, ((0, 4), (1, 8)))
    chosen = draw_chosen(jax.random.fold_in(seeds[7], 71), 0)
    counts = draw_counts(jax.random.fold_in(seeds[7], 71), 0)
    gate_codes = with_ends(jax.random.randint(seeds[6], (EXPERTS, N_DP, SLOTS), 16384, 65537), jax.random.fold_in(seeds[6], 1), 16384, 65536).astype(jnp.int32)
    return dict(tokens=tokens, w_gate=w_gate, w_up=w_up, w_down=w_down, chosen=chosen, counts=counts, gate_codes=gate_codes)


def reference(tokens, w_gate, w_up, w_down, chosen, counts, gate_codes):
    shards = tokens.reshape(N_DP, TOK_DEV, D)
    shard_ids = jnp.arange(N_DP, dtype=jnp.int32)[:, None]
    slot_ids = jnp.arange(SLOTS, dtype=jnp.int32)[None, :]

    def one_expert(total, inputs):
        gate_w, up_w, down_w, picks, live, codes = inputs
        fetched = shards[shard_ids, picks].reshape(N_DP * SLOTS, D)
        gate_proj = jnp.dot(fetched, gate_w, preferred_element_type=jnp.float32)
        up_proj = jnp.dot(fetched, up_w, preferred_element_type=jnp.float32)
        hidden = (jax.nn.silu(gate_proj) * up_proj).astype(jnp.bfloat16)
        expert_out = jnp.dot(hidden, down_w, preferred_element_type=jnp.float32).reshape(N_DP, SLOTS, D)
        weight = codes.astype(jnp.float32) / 65536.0 * (slot_ids < live[:, None]).astype(jnp.float32)
        total = total.at[shard_ids, picks].add(expert_out * weight[:, :, None])
        return total, None

    start = jnp.zeros((N_DP, TOK_DEV, D), jnp.float32)
    total, _ = lax.scan(one_expert, start, (w_gate, w_up, w_down, chosen, counts, gate_codes))
    return total.reshape(N_DP * TOK_DEV, D).astype(jnp.bfloat16)
```

```python
import functools

import jax
import jax.numpy as jnp
from jax import lax
from jax.experimental import pallas as pl
from jax.experimental.pallas import tpu as pltpu
from jax.sharding import PartitionSpec as P

LANES = 128
TILE = 16
MESH = pl.DeviceIdType.MESH


def iota(shape, dim):
    return lax.broadcasted_iota(jnp.int32, shape, dim)


def one_hot(hit):
    return jnp.where(hit, 1.0, 0.0).astype(jnp.bfloat16)


def matmul(a, b):
    return jnp.dot(a, b, preferred_element_type=jnp.float32)


def moe_kernel(
    n_dp, n_ex,
    chosen, counts, codes, tokens, w_gate, w_up, w_down, out,
    tok, wg, wu, wd, pick, gathered, lhs, gate, up, hidden, back_perm, ready, landed,
    tok_sem, wg_sem, wu_sem, wd_sem, pick_send, pick_recv, back_send, back_recv,
):
    n = n_dp * n_ex
    my_dp, my_ex = lax.axis_index("dp"), lax.axis_index("expert")
    me = my_dp * n_ex + my_ex
    slots = chosen.shape[2]
    rows = n_dp * slots
    per_row = TILE // slots
    depth = pick.shape[1]
    n_tok = tok.shape[0]
    width = wd.shape[2]
    pieces = width // LANES
    block = ready.shape[2]

    tok_copy = pltpu.make_async_copy(tokens, tok, tok_sem)
    tok_copy.start()

    def in_copies(k):
        part = pl.ds(k * depth, depth)
        return (
            pltpu.make_async_copy(w_gate.at[0, part, :], wg.at[k], wg_sem.at[k]),
            pltpu.make_async_copy(w_up.at[0, part, :], wu.at[k], wu_sem.at[k]),
        )

    def feature_block(i):
        return lax.rem(my_ex + 1 + i, n_ex)

    def down_copy(i):
        part = pl.ds(pl.multiple_of(feature_block(i) * width, LANES), width)
        return pltpu.make_async_copy(w_down.at[0, :, part], wd.at[i], wd_sem.at[i])

    @pl.loop(0, per_row)
    def _(k):
        for copy in in_copies(k):
            copy.start()

    @pl.loop(0, n_ex)
    def _(i):
        down_copy(i).start()

    barrier = pltpu.get_barrier_semaphore()

    @pl.loop(1, n)
    def _(k):
        other = lax.rem(me + k, n)
        pl.semaphore_signal(
            barrier, inc=1, device_id=(other // n_ex, lax.rem(other, n_ex)), device_id_type=MESH
        )

    row = iota((TILE, n_tok), 0)
    named = jnp.zeros((TILE, n_tok), jnp.int32)
    for j in range(slots):
        named = jnp.where(row // per_row == j, chosen[my_ex, 0, j], named)
    hit = named == iota((TILE, n_tok), 1)
    tok_copy.wait()
    picked = jnp.zeros((TILE, depth), jnp.float32)
    for k in range(per_row):
        select = one_hot(jnp.logical_and(hit, row % per_row == k))
        picked += matmul(select, tok[:, k * depth:(k + 1) * depth])
    pick[...] = picked.astype(jnp.bfloat16)

    pl.semaphore_wait(barrier, n - 1)

    @pl.loop(1, n_dp)
    def _(k):
        pltpu.make_async_remote_copy(
            src_ref=pick, dst_ref=gathered.at[my_dp],
            send_sem=pick_send, recv_sem=pick_recv,
            device_id=(lax.rem(my_dp + k, n_dp), my_ex), device_id_type=MESH,
        ).start()

    pltpu.make_async_copy(pick, gathered.at[my_dp], pick_recv).start()

    gate[...] = jnp.zeros_like(gate)
    up[...] = jnp.zeros_like(up)
    to = iota(back_perm.shape, 0)
    source = iota(back_perm.shape, 1)
    place = to % block
    back_perm[...] = one_hot(
        jnp.logical_and(
            source == (place % pieces) * rows + (to // block) * slots + place // pieces,
            place < slots * pieces,
        )
    )

    weight_rows = n_ex * block
    wrow = iota((weight_rows, LANES), 0)
    wslot = (wrow // block) * slots + (wrow % block) // pieces
    wvalid = wrow % block < slots * pieces
    weight = jnp.zeros((weight_rows, LANES), jnp.float32)
    column = iota((n_tok, weight_rows), 1)
    cslot = (column // block) * slots + (column % block) // pieces
    cvalid = column % block < slots * pieces
    token_of = jnp.full((n_tok, weight_rows), -1, jnp.int32)
    for e in range(n_ex):
        for j in range(slots):
            own = codes[e, 0, j].astype(jnp.float32) / 65536.0
            own = jnp.where(j < counts[e, 0], own, 0.0)
            weight = jnp.where(jnp.logical_and(wvalid, wslot == e * slots + j), own, weight)
            token_of = jnp.where(
                jnp.logical_and(cvalid, cslot == e * slots + j), chosen[e, 0, j], token_of
            )
    scatter = one_hot(token_of == iota((n_tok, weight_rows), 0))

    pltpu.make_async_copy(gathered, gathered, pick_recv).wait()

    stacked = gathered[...].reshape(n_dp * TILE, depth)
    to = iota((rows, n_dp * TILE), 0)
    source = iota((rows, n_dp * TILE), 1)
    first = (to // slots) * TILE + (to % slots) * per_row
    for k in range(per_row):
        lhs[k] = matmul(one_hot(source == first + k), stacked).astype(jnp.bfloat16)

    @pl.loop(0, per_row)
    def _(k):
        for copy in in_copies(k):
            copy.wait()
        gate[...] += matmul(lhs[k], wg[k])
        up[...] += matmul(lhs[k], wu[k])

    value = gate[...]
    hidden[...] = (value / (1.0 + jnp.exp(-value)) * up[...]).astype(jnp.bfloat16)

    @pl.loop(0, n_ex)
    def _(i):
        f = feature_block(i)
        down_copy(i).wait()
        part = matmul(hidden[...], wd[i]).astype(jnp.bfloat16)
        piled = jnp.concatenate(
            [part[:, c * LANES:(c + 1) * LANES] for c in range(pieces)], axis=0
        )
        ready[i] = matmul(back_perm[...], piled).astype(jnp.bfloat16).reshape(n_dp, block, LANES)

        @pl.loop(0, n_dp)
        def _(k):
            s = lax.rem(my_dp + 1 + k, n_dp)
            own = jnp.logical_and(s == my_dp, f == my_ex)

            @pl.when(jnp.logical_not(own))
            def _():
                pltpu.make_async_remote_copy(
                    src_ref=ready.at[i, s], dst_ref=landed.at[me],
                    send_sem=back_send, recv_sem=back_recv,
                    device_id=(s, f), device_id_type=MESH,
                ).start()

            @pl.when(own)
            def _():
                pltpu.make_async_copy(ready.at[i, s], landed.at[me], back_recv).start()

    pltpu.make_async_copy(landed, landed, back_recv).wait()

    def add(s, total):
        held = landed[pl.ds(s * n_ex, n_ex)].astype(jnp.float32)
        return total + held.reshape(weight_rows, LANES)

    total = lax.fori_loop(0, n_dp, add, jnp.zeros((weight_rows, LANES), jnp.float32), unroll=n_dp <= 8)
    total = total * weight
    high = total.astype(jnp.bfloat16)
    rest = total - high.astype(jnp.float32)
    low = rest.astype(jnp.bfloat16)
    spot = (wrow % block) % pieces
    for c in range(pieces):
        mine = spot == c
        result = matmul(scatter, jnp.where(mine, high.astype(jnp.float32), 0.0).astype(jnp.bfloat16))
        result += matmul(scatter, jnp.where(mine, low.astype(jnp.float32), 0.0).astype(jnp.bfloat16))
        out[:, c * LANES:(c + 1) * LANES] = result.astype(out.dtype)

    sent = gathered.at[pl.ds(0, n_dp - 1)]
    pltpu.make_async_copy(sent, sent, pick_send).wait()
    sent = landed.at[pl.ds(0, n - 1)]
    pltpu.make_async_copy(sent, sent, back_send).wait()


def on_device(n_dp, n_ex, tokens, w_gate, w_up, w_down, chosen, counts, gate_codes):
    n_tok, d = tokens.shape
    hidden_units = w_gate.shape[2]
    slots = chosen.shape[2]
    rows = n_dp * slots
    per_row = TILE // slots
    depth = d // per_row
    width = d // n_ex
    pieces = width // LANES
    block = -(-slots * pieces // TILE) * TILE
    n = n_dp * n_ex
    bf16, f32 = jnp.bfloat16, jnp.float32
    dma = pltpu.SemaphoreType.DMA
    hbm = pl.BlockSpec(memory_space=pl.ANY)
    smem = pl.BlockSpec(memory_space=pltpu.SMEM)
    return pl.pallas_call(
        functools.partial(moe_kernel, n_dp, n_ex),
        out_shape=jax.ShapeDtypeStruct((n_tok, width), bf16),
        in_specs=[smem] * 3 + [hbm] * 4,
        out_specs=pl.BlockSpec(memory_space=pltpu.VMEM),
        scratch_shapes=[
            pltpu.VMEM((n_tok, d), bf16),
            pltpu.VMEM((per_row, depth, hidden_units), bf16),
            pltpu.VMEM((per_row, depth, hidden_units), bf16),
            pltpu.VMEM((n_ex, hidden_units, width), bf16),
            pltpu.VMEM((TILE, depth), bf16),
            pltpu.VMEM((n_dp, TILE, depth), bf16),
            pltpu.VMEM((per_row, rows, depth), bf16),
            pltpu.VMEM((rows, hidden_units), f32),
            pltpu.VMEM((rows, hidden_units), f32),
            pltpu.VMEM((rows, hidden_units), bf16),
            pltpu.VMEM((n_dp * block, pieces * rows), bf16),
            pltpu.VMEM((n_ex, n_dp, block, LANES), bf16),
            pltpu.VMEM((n, block, LANES), bf16),
            dma,
            dma((per_row,)),
            dma((per_row,)),
            dma((n_ex,)),
            dma,
            dma,
            dma,
            dma,
        ],
        compiler_params=pltpu.CompilerParams(
            collective_id=0, has_side_effects=True, vmem_limit_bytes=48 * 1024 * 1024
        ),
        cost_estimate=pl.CostEstimate(
            flops=6 * rows * d * hidden_units,
            bytes_accessed=6 * d * hidden_units,
            transcendentals=rows * hidden_units,
        ),
    )(chosen, counts, gate_codes, tokens, w_gate, w_up, w_down)


def solution(mesh):
    placed = (
        P("dp", None),
        P("expert", None, "dp"),
        P("expert", None, "dp"),
        P("expert", "dp", None),
        P(None, "dp", None),
        P(None, "dp"),
        P(None, "dp", None),
    )
    return jax.shard_map(
        functools.partial(on_device, mesh.shape["dp"], mesh.shape["expert"]),
        mesh=mesh, in_specs=placed, out_specs=P("dp", "expert"), check_vma=False,
    )
```

```python
import functools

import jax
import jax.numpy as jnp
from jax import lax
from jax.experimental import pallas as pl
from jax.experimental.pallas import tpu as pltpu
from jax.sharding import PartitionSpec as P

LANES = 128
TILE = 16
MESH = pl.DeviceIdType.MESH


def iota(shape, dim):
    return lax.broadcasted_iota(jnp.int32, shape, dim)


def one_hot(hit):
    return jnp.where(hit, 1.0, 0.0).astype(jnp.bfloat16)


def matmul(a, b):
    return jnp.dot(a, b, preferred_element_type=jnp.float32)


def moe_kernel(
    n_dp, n_ex,
    chosen_hbm, counts_hbm, codes_hbm, tokens, w_gate, w_up, w_down, out,
    chosen, counts, codes, tok, wg, wu, wd, pick, gathered, lhs, gate, up, hidden, back_perm, ready, landed,
    slot_sem, tok_sem, wg_sem, wu_sem, wd_sem, pick_send, pick_recv, back_send, back_recv,
):
    n = n_dp * n_ex
    my_dp, my_ex = lax.axis_index("dp"), lax.axis_index("expert")
    me = my_dp * n_ex + my_ex
    slots = chosen.shape[1]
    rows = n_dp * slots
    per_row = TILE // slots
    half = pick.shape[2]
    depth = wg.shape[1]
    n_tok = tok.shape[0]
    width = wd.shape[2]
    pieces = width // LANES
    block = ready.shape[2]

    tok_copy = pltpu.make_async_copy(tokens, tok, tok_sem)
    tok_copy.start()
    slot_copies = [
        pltpu.make_async_copy(source, target, slot_sem.at[i])
        for i, (source, target) in enumerate(
            ((chosen_hbm, chosen), (counts_hbm, counts), (codes_hbm, codes))
        )
    ]
    for copy in slot_copies:
        copy.start()

    barrier = pltpu.get_barrier_semaphore()

    @pl.loop(1, n)
    def _(k):
        other = lax.rem(me + k, n)
        pl.semaphore_signal(
            barrier, inc=1, device_id=(other // n_ex, lax.rem(other, n_ex)), device_id_type=MESH
        )

    def in_copies(k):
        part = pl.ds(k * depth, depth)
        return (
            pltpu.make_async_copy(w_gate.at[0, part, :], wg.at[k], wg_sem.at[k]),
            pltpu.make_async_copy(w_up.at[0, part, :], wu.at[k], wu_sem.at[k]),
        )

    def feature_block(i):
        return lax.rem(my_ex + 1 + i, n_ex)

    def down_copy(i):
        part = pl.ds(pl.multiple_of(feature_block(i) * width, LANES), width)
        return pltpu.make_async_copy(w_down.at[0, :, part], wd.at[i], wd_sem.at[i])

    @pl.loop(0, per_row)
    def _(k):
        for copy in in_copies(k):
            copy.start()

    @pl.loop(0, n_ex)
    def _(i):
        down_copy(i).start()

    row = iota((TILE, n_tok), 0)
    named = jnp.zeros((TILE, n_tok), jnp.int32)
    slot_copies[0].wait()
    for j in range(slots):
        named = jnp.where(row // per_row == j, chosen[0, j, my_ex], named)
    hit = named == iota((TILE, n_tok), 1)
    select = [one_hot(jnp.logical_and(hit, row % per_row == k)) for k in range(per_row)]
    tok_copy.wait()
    for h in range(2):
        picked = jnp.zeros((TILE, half), jnp.float32)
        for k in range(per_row):
            start = (h * per_row + k) * half
            picked += matmul(select[k], tok[:, start:start + half])
        pick[h] = picked.astype(jnp.bfloat16)

    pl.semaphore_wait(barrier, n - 1)

    for h in range(2):
        @pl.loop(1, n_dp)
        def _(k):
            pltpu.make_async_remote_copy(
                src_ref=pick.at[h], dst_ref=gathered.at[h, my_dp],
                send_sem=pick_send, recv_sem=pick_recv.at[h],
                device_id=(lax.rem(my_dp + k, n_dp), my_ex), device_id_type=MESH,
            ).start()

        pltpu.make_async_copy(pick.at[h], gathered.at[h, my_dp], pick_recv.at[h]).start()

    gate[...] = jnp.zeros_like(gate)
    up[...] = jnp.zeros_like(up)
    to = iota(back_perm.shape, 0)
    source = iota(back_perm.shape, 1)
    place = to % block
    back_perm[...] = one_hot(
        jnp.logical_and(
            source == (place % pieces) * rows + (to // block) * slots + place // pieces,
            place < slots * pieces,
        )
    )

    weight_rows = n_ex * block
    wrow = iota((weight_rows, LANES), 0)
    wslot = (wrow // block) * slots + (wrow % block) // pieces
    wvalid = wrow % block < slots * pieces
    weight = jnp.zeros((weight_rows, LANES), jnp.float32)
    column = iota((n_tok, weight_rows), 1)
    cslot = (column // block) * slots + (column % block) // pieces
    cvalid = column % block < slots * pieces
    token_of = jnp.full((n_tok, weight_rows), -1, jnp.int32)
    for copy in slot_copies[1:]:
        copy.wait()
    for e in range(n_ex):
        for j in range(slots):
            own = codes[0, j, e].astype(jnp.float32) / 65536.0
            own = jnp.where(j < counts[0, e], own, 0.0)
            weight = jnp.where(jnp.logical_and(wvalid, wslot == e * slots + j), own, weight)
            token_of = jnp.where(
                jnp.logical_and(cvalid, cslot == e * slots + j), chosen[0, j, e], token_of
            )
    scatter = one_hot(token_of == iota((n_tok, weight_rows), 0))

    to = iota((rows, n_dp * TILE), 0)
    source = iota((rows, n_dp * TILE), 1)
    first = (to // slots) * TILE + (to % slots) * per_row
    spread = [one_hot(source == first + k) for k in range(per_row)]
    for h in range(2):
        pltpu.make_async_copy(gathered.at[h], gathered.at[h], pick_recv.at[h]).wait()
        stacked = gathered[h].reshape(n_dp * TILE, half)
        for k in range(per_row):
            q = h * per_row + k
            lhs[q // 2, :, (q % 2) * half:(q % 2 + 1) * half] = (
                matmul(spread[k], stacked).astype(jnp.bfloat16)
            )

        @pl.loop(h * per_row // 2, (h + 1) * per_row // 2)
        def _(k):
            for copy in in_copies(k):
                copy.wait()
            gate[...] += matmul(lhs[k], wg[k])
            up[...] += matmul(lhs[k], wu[k])

    value = gate[...]
    hidden[...] = (value / (1.0 + jnp.exp(-value)) * up[...]).astype(jnp.bfloat16)

    @pl.loop(0, n_ex)
    def _(i):
        f = feature_block(i)
        down_copy(i).wait()
        part = matmul(hidden[...], wd[i]).astype(jnp.bfloat16)
        piled = jnp.concatenate(
            [part[:, c * LANES:(c + 1) * LANES] for c in range(pieces)], axis=0
        )
        ready[i] = matmul(back_perm[...], piled).astype(jnp.bfloat16).reshape(n_dp, block, LANES)

        @pl.loop(0, n_dp)
        def _(k):
            s = lax.rem(my_dp + 1 + k, n_dp)
            own = jnp.logical_and(s == my_dp, f == my_ex)

            @pl.when(jnp.logical_not(own))
            def _():
                pltpu.make_async_remote_copy(
                    src_ref=ready.at[i, s], dst_ref=landed.at[me],
                    send_sem=back_send, recv_sem=back_recv,
                    device_id=(s, f), device_id_type=MESH,
                ).start()

            @pl.when(own)
            def _():
                pltpu.make_async_copy(ready.at[i, s], landed.at[me], back_recv).start()

    pltpu.make_async_copy(landed, landed, back_recv).wait()

    def add(s, total):
        held = landed[pl.ds(s * n_ex, n_ex)].astype(jnp.float32)
        return total + held.reshape(weight_rows, LANES)

    total = lax.fori_loop(0, n_dp, add, jnp.zeros((weight_rows, LANES), jnp.float32), unroll=n_dp <= 8)
    total = total * weight
    high = total.astype(jnp.bfloat16)
    rest = total - high.astype(jnp.float32)
    low = rest.astype(jnp.bfloat16)
    spot = (wrow % block) % pieces
    for c in range(pieces):
        mine = spot == c
        result = matmul(scatter, jnp.where(mine, high.astype(jnp.float32), 0.0).astype(jnp.bfloat16))
        result += matmul(scatter, jnp.where(mine, low.astype(jnp.float32), 0.0).astype(jnp.bfloat16))
        out[:, c * LANES:(c + 1) * LANES] = result.astype(out.dtype)

    sent = gathered.at[:, pl.ds(0, n_dp - 1)]
    pltpu.make_async_copy(sent, sent, pick_send).wait()
    sent = landed.at[pl.ds(0, n - 1)]
    pltpu.make_async_copy(sent, sent, back_send).wait()


def on_device(n_dp, n_ex, tokens, w_gate, w_up, w_down, chosen, counts, gate_codes):
    n_tok, d = tokens.shape
    hidden_units = w_gate.shape[2]
    slots = chosen.shape[2]
    rows = n_dp * slots
    per_row = TILE // slots
    depth = d // per_row
    width = d // n_ex
    pieces = width // LANES
    block = -(-slots * pieces // TILE) * TILE
    n = n_dp * n_ex
    bf16, f32 = jnp.bfloat16, jnp.float32
    dma = pltpu.SemaphoreType.DMA
    hbm = pl.BlockSpec(memory_space=pltpu.HBM)
    return pl.pallas_call(
        functools.partial(moe_kernel, n_dp, n_ex),
        out_shape=jax.ShapeDtypeStruct((n_tok, width), bf16),
        in_specs=[hbm] * 7,
        out_specs=pl.BlockSpec(memory_space=pltpu.VMEM),
        scratch_shapes=[
            pltpu.SMEM((1, slots, n_ex), jnp.int32),
            pltpu.SMEM((1, n_ex), jnp.int32),
            pltpu.SMEM((1, slots, n_ex), jnp.int32),
            pltpu.VMEM((n_tok, d), bf16),
            pltpu.VMEM((per_row, depth, hidden_units), bf16),
            pltpu.VMEM((per_row, depth, hidden_units), bf16),
            pltpu.VMEM((n_ex, hidden_units, width), bf16),
            pltpu.VMEM((2, TILE, depth // 2), bf16),
            pltpu.VMEM((2, n_dp, TILE, depth // 2), bf16),
            pltpu.VMEM((per_row, rows, depth), bf16),
            pltpu.VMEM((rows, hidden_units), f32),
            pltpu.VMEM((rows, hidden_units), f32),
            pltpu.VMEM((rows, hidden_units), bf16),
            pltpu.VMEM((n_dp * block, pieces * rows), bf16),
            pltpu.VMEM((n_ex, n_dp, block, LANES), bf16),
            pltpu.VMEM((n, block, LANES), bf16),
            dma((3,)),
            dma,
            dma((per_row,)),
            dma((per_row,)),
            dma((n_ex,)),
            dma,
            dma((2,)),
            dma,
            dma,
        ],
        compiler_params=pltpu.CompilerParams(
            collective_id=0, has_side_effects=True, vmem_limit_bytes=60 * 1024 * 1024
        ),
        cost_estimate=pl.CostEstimate(
            flops=6 * rows * d * hidden_units,
            bytes_accessed=6 * d * hidden_units,
            transcendentals=rows * hidden_units,
        ),
    )(chosen.transpose(1, 2, 0), counts.T, gate_codes.transpose(1, 2, 0), tokens, w_gate, w_up, w_down)


def solution(mesh):
    placed = (
        P("dp", None),
        P("expert", None, "dp"),
        P("expert", None, "dp"),
        P("expert", "dp", None),
        P(None, "dp", None),
        P(None, "dp"),
        P(None, "dp", None),
    )
    return jax.shard_map(
        functools.partial(on_device, mesh.shape["dp"], mesh.shape["expert"]),
        mesh=mesh, in_specs=placed, out_specs=P("dp", "expert"), check_vma=False,
    )
```

```python
import functools

import jax
import jax.numpy as jnp
from jax import lax
from jax.experimental import pallas as pl
from jax.experimental.pallas import tpu as pltpu
from jax.sharding import PartitionSpec as P

LANES = 128
TILE = 16
MESH = pl.DeviceIdType.MESH


def iota(shape, dim):
    return lax.broadcasted_iota(jnp.int32, shape, dim)


def one_hot(hit):
    return jnp.where(hit, 1.0, 0.0).astype(jnp.bfloat16)


def matmul(a, b):
    return jnp.dot(a, b, preferred_element_type=jnp.float32)


def moe_kernel(
    n_dp, n_ex,
    chosen_hbm, counts_hbm, codes_hbm, tokens, w_gate, w_up, w_down, out,
    chosen, counts, codes, tok, wg, wu, wd, pick, gathered, lhs, gate, up, hidden, back_perm, ready, landed,
    slot_sem, tok_sem, wg_sem, wu_sem, wd_sem, pick_send, pick_recv, back_send, back_recv, column_sem,
):
    n = n_dp * n_ex
    my_dp, my_ex = lax.axis_index("dp"), lax.axis_index("expert")
    me = my_dp * n_ex + my_ex
    slots = chosen.shape[1]
    rows = n_dp * slots
    per_row = TILE // slots
    half = pick.shape[2]
    depth = wg.shape[1]
    n_tok = tok.shape[0]
    width = wd.shape[2]
    pieces = width // LANES
    block = ready.shape[2]

    tok_copy = pltpu.make_async_copy(tokens, tok, tok_sem)
    tok_copy.start()
    slot_copies = [
        pltpu.make_async_copy(source, target, slot_sem.at[i])
        for i, (source, target) in enumerate(
            ((chosen_hbm, chosen), (counts_hbm, counts), (codes_hbm, codes))
        )
    ]
    for copy in slot_copies:
        copy.start()

    barrier = pltpu.get_barrier_semaphore()

    @pl.loop(1, n_dp)
    def _(k):
        pl.semaphore_signal(
            barrier, inc=1, device_id=(lax.rem(my_dp + k, n_dp), my_ex), device_id_type=MESH
        )

    @pl.loop(1, n_ex)
    def _(k):
        pl.semaphore_signal(
            barrier, inc=1, device_id=(my_dp, lax.rem(my_ex + k, n_ex)), device_id_type=MESH
        )

    def in_copies(k):
        part = pl.ds(k * depth, depth)
        return (
            pltpu.make_async_copy(w_gate.at[0, part, :], wg.at[k], wg_sem.at[k]),
            pltpu.make_async_copy(w_up.at[0, part, :], wu.at[k], wu_sem.at[k]),
        )

    def feature_block(i):
        return lax.rem(my_ex + 1 + i, n_ex)

    def down_copy(i):
        part = pl.ds(pl.multiple_of(feature_block(i) * width, LANES), width)
        return pltpu.make_async_copy(w_down.at[0, :, part], wd.at[i], wd_sem.at[i])

    @pl.loop(0, per_row)
    def _(k):
        for copy in in_copies(k):
            copy.start()

    @pl.loop(0, n_ex)
    def _(i):
        down_copy(i).start()

    row = iota((TILE, n_tok), 0)
    named = jnp.zeros((TILE, n_tok), jnp.int32)
    slot_copies[0].wait()
    for j in range(slots):
        named = jnp.where(row // per_row == j, chosen[0, j, my_ex], named)
    hit = named == iota((TILE, n_tok), 1)
    select = [one_hot(jnp.logical_and(hit, row % per_row == k)) for k in range(per_row)]
    tok_copy.wait()
    for h in range(2):
        picked = jnp.zeros((TILE, half), jnp.float32)
        for k in range(per_row):
            start = (h * per_row + k) * half
            picked += matmul(select[k], tok[:, start:start + half])
        pick[h] = picked.astype(jnp.bfloat16)

    pl.semaphore_wait(barrier, n_dp - 1 + n_ex - 1)

    for h in range(2):
        @pl.loop(1, n_dp)
        def _(k):
            pltpu.make_async_remote_copy(
                src_ref=pick.at[h], dst_ref=gathered.at[h, my_dp],
                send_sem=pick_send, recv_sem=pick_recv.at[h],
                device_id=(lax.rem(my_dp + k, n_dp), my_ex), device_id_type=MESH,
            ).start()

        pltpu.make_async_copy(pick.at[h], gathered.at[h, my_dp], pick_recv.at[h]).start()

    @pl.loop(1, n_ex)
    def _(k):
        pl.semaphore_signal(
            column_sem, inc=1, device_id=(my_dp, lax.rem(my_ex + k, n_ex)), device_id_type=MESH
        )

    gate[...] = jnp.zeros_like(gate)
    up[...] = jnp.zeros_like(up)
    to = iota(back_perm.shape, 0)
    source = iota(back_perm.shape, 1)
    place = to % block
    back_perm[...] = one_hot(
        jnp.logical_and(
            source == (place % pieces) * rows + (to // block) * slots + place // pieces,
            place < slots * pieces,
        )
    )

    weight_rows = n_ex * block
    wrow = iota((weight_rows, LANES), 0)
    wslot = (wrow // block) * slots + (wrow % block) // pieces
    wvalid = wrow % block < slots * pieces
    weight = jnp.zeros((weight_rows, LANES), jnp.float32)
    column = iota((n_tok, weight_rows), 1)
    cslot = (column // block) * slots + (column % block) // pieces
    cvalid = column % block < slots * pieces
    token_of = jnp.full((n_tok, weight_rows), -1, jnp.int32)
    for copy in slot_copies[1:]:
        copy.wait()
    for e in range(n_ex):
        for j in range(slots):
            own = codes[0, j, e].astype(jnp.float32) / 65536.0
            own = jnp.where(j < counts[0, e], own, 0.0)
            weight = jnp.where(jnp.logical_and(wvalid, wslot == e * slots + j), own, weight)
            token_of = jnp.where(
                jnp.logical_and(cvalid, cslot == e * slots + j), chosen[0, j, e], token_of
            )
    scatter = one_hot(token_of == iota((n_tok, weight_rows), 0))

    to = iota((rows, n_dp * TILE), 0)
    source = iota((rows, n_dp * TILE), 1)
    first = (to // slots) * TILE + (to % slots) * per_row
    spread = [one_hot(source == first + k) for k in range(per_row)]
    for h in range(2):
        pltpu.make_async_copy(gathered.at[h], gathered.at[h], pick_recv.at[h]).wait()
        stacked = gathered[h].reshape(n_dp * TILE, half)
        for k in range(per_row):
            q = h * per_row + k
            lhs[q // 2, :, (q % 2) * half:(q % 2 + 1) * half] = (
                matmul(spread[k], stacked).astype(jnp.bfloat16)
            )

        @pl.loop(h * per_row // 2, (h + 1) * per_row // 2)
        def _(k):
            for copy in in_copies(k):
                copy.wait()
            gate[...] += matmul(lhs[k], wg[k])
            up[...] += matmul(lhs[k], wu[k])

    pl.semaphore_wait(column_sem, n_ex - 1)
    value = gate[...]
    hidden[...] = (value / (1.0 + jnp.exp(-value)) * up[...]).astype(jnp.bfloat16)

    @pl.loop(0, n_ex)
    def _(i):
        f = feature_block(i)
        down_copy(i).wait()
        part = matmul(hidden[...], wd[i]).astype(jnp.bfloat16)
        piled = jnp.concatenate(
            [part[:, c * LANES:(c + 1) * LANES] for c in range(pieces)], axis=0
        )
        ready[i] = matmul(back_perm[...], piled).astype(jnp.bfloat16).reshape(n_dp, block, LANES)

        @pl.loop(0, n_dp)
        def _(k):
            s = lax.rem(my_dp + 1 + k, n_dp)
            own = jnp.logical_and(s == my_dp, f == my_ex)

            @pl.when(jnp.logical_not(own))
            def _():
                pltpu.make_async_remote_copy(
                    src_ref=ready.at[i, s], dst_ref=landed.at[me],
                    send_sem=back_send, recv_sem=back_recv,
                    device_id=(s, f), device_id_type=MESH,
                ).start()

            @pl.when(own)
            def _():
                pltpu.make_async_copy(ready.at[i, s], landed.at[me], back_recv).start()

    pltpu.make_async_copy(landed, landed, back_recv).wait()

    def add(s, total):
        held = landed[pl.ds(s * n_ex, n_ex)].astype(jnp.float32)
        return total + held.reshape(weight_rows, LANES)

    total = lax.fori_loop(0, n_dp, add, jnp.zeros((weight_rows, LANES), jnp.float32), unroll=n_dp <= 8)
    total = total * weight
    high = total.astype(jnp.bfloat16)
    rest = total - high.astype(jnp.float32)
    low = rest.astype(jnp.bfloat16)
    spot = (wrow % block) % pieces
    for c in range(pieces):
        mine = spot == c
        result = matmul(scatter, jnp.where(mine, high.astype(jnp.float32), 0.0).astype(jnp.bfloat16))
        result += matmul(scatter, jnp.where(mine, low.astype(jnp.float32), 0.0).astype(jnp.bfloat16))
        out[:, c * LANES:(c + 1) * LANES] = result.astype(out.dtype)

    sent = gathered.at[:, pl.ds(0, n_dp - 1)]
    pltpu.make_async_copy(sent, sent, pick_send).wait()
    sent = landed.at[pl.ds(0, n - 1)]
    pltpu.make_async_copy(sent, sent, back_send).wait()


def on_device(n_dp, n_ex, tokens, w_gate, w_up, w_down, chosen, counts, gate_codes):
    n_tok, d = tokens.shape
    hidden_units = w_gate.shape[2]
    slots = chosen.shape[2]
    rows = n_dp * slots
    per_row = TILE // slots
    depth = d // per_row
    width = d // n_ex
    pieces = width // LANES
    block = -(-slots * pieces // TILE) * TILE
    n = n_dp * n_ex
    bf16, f32 = jnp.bfloat16, jnp.float32
    dma = pltpu.SemaphoreType.DMA
    hbm = pl.BlockSpec(memory_space=pltpu.HBM)
    return pl.pallas_call(
        functools.partial(moe_kernel, n_dp, n_ex),
        out_shape=jax.ShapeDtypeStruct((n_tok, width), bf16),
        in_specs=[hbm] * 7,
        out_specs=pl.BlockSpec(memory_space=pltpu.VMEM),
        scratch_shapes=[
            pltpu.SMEM((1, slots, n_ex), jnp.int32),
            pltpu.SMEM((1, n_ex), jnp.int32),
            pltpu.SMEM((1, slots, n_ex), jnp.int32),
            pltpu.VMEM((n_tok, d), bf16),
            pltpu.VMEM((per_row, depth, hidden_units), bf16),
            pltpu.VMEM((per_row, depth, hidden_units), bf16),
            pltpu.VMEM((n_ex, hidden_units, width), bf16),
            pltpu.VMEM((2, TILE, depth // 2), bf16),
            pltpu.VMEM((2, n_dp, TILE, depth // 2), bf16),
            pltpu.VMEM((per_row, rows, depth), bf16),
            pltpu.VMEM((rows, hidden_units), f32),
            pltpu.VMEM((rows, hidden_units), f32),
            pltpu.VMEM((rows, hidden_units), bf16),
            pltpu.VMEM((n_dp * block, pieces * rows), bf16),
            pltpu.VMEM((n_ex, n_dp, block, LANES), bf16),
            pltpu.VMEM((n, block, LANES), bf16),
            dma((3,)),
            dma,
            dma((per_row,)),
            dma((per_row,)),
            dma((n_ex,)),
            dma,
            dma((2,)),
            dma,
            dma,
            pltpu.SemaphoreType.REGULAR,
        ],
        compiler_params=pltpu.CompilerParams(
            collective_id=0, has_side_effects=True, vmem_limit_bytes=60 * 1024 * 1024
        ),
        cost_estimate=pl.CostEstimate(
            flops=6 * rows * d * hidden_units,
            bytes_accessed=6 * d * hidden_units,
            transcendentals=rows * hidden_units,
        ),
    )(chosen.transpose(1, 2, 0), counts.T, gate_codes.transpose(1, 2, 0), tokens, w_gate, w_up, w_down)


def solution(mesh):
    placed = (
        P("dp", None),
        P("expert", None, "dp"),
        P("expert", None, "dp"),
        P("expert", "dp", None),
        P(None, "dp", None),
        P(None, "dp"),
        P(None, "dp", None),
    )
    return jax.shard_map(
        functools.partial(on_device, mesh.shape["dp"], mesh.shape["expert"]),
        mesh=mesh, in_specs=placed, out_specs=P("dp", "expert"), check_vma=False,
    )
```

```python
import functools

import jax
import jax.numpy as jnp
from jax import lax
from jax.experimental import pallas as pl
from jax.experimental.pallas import tpu as pltpu
from jax.sharding import PartitionSpec as P

LANES = 128
TILE = 16
PARTS = 4
MESH = pl.DeviceIdType.MESH


def iota(shape, dim):
    return lax.broadcasted_iota(jnp.int32, shape, dim)


def one_hot(hit):
    return jnp.where(hit, 1.0, 0.0).astype(jnp.bfloat16)


def matmul(a, b):
    return jnp.dot(a, b, preferred_element_type=jnp.float32)


def moe_kernel(
    n_dp, n_ex,
    chosen_hbm, counts_hbm, codes_hbm, tokens, w_gate, w_up, w_down, out,
    chosen, counts, codes, tok, wg, wu, wd, pick, gathered, lhs, gate, up, hidden, back_perm, ready, landed,
    slot_sem, tok_sem, wg_sem, wu_sem, wd_sem, pick_send, pick_recv, back_send, back_recv, column_sem,
):
    n = n_dp * n_ex
    my_dp, my_ex = lax.axis_index("dp"), lax.axis_index("expert")
    me = my_dp * n_ex + my_ex
    slots = chosen.shape[1]
    rows = n_dp * slots
    per_row = TILE // slots
    half = pick.shape[2]
    depth = wg.shape[1]
    n_tok = tok.shape[0]
    width = wd.shape[2]
    pieces = width // LANES
    block = ready.shape[2]

    tok_copy = pltpu.make_async_copy(tokens, tok, tok_sem)
    tok_copy.start()
    slot_copies = [
        pltpu.make_async_copy(source, target, slot_sem.at[i])
        for i, (source, target) in enumerate(
            ((chosen_hbm, chosen), (counts_hbm, counts), (codes_hbm, codes))
        )
    ]
    for copy in slot_copies:
        copy.start()

    barrier = pltpu.get_barrier_semaphore()

    @pl.loop(1, n_dp)
    def _(k):
        pl.semaphore_signal(
            barrier, inc=1, device_id=(lax.rem(my_dp + k, n_dp), my_ex), device_id_type=MESH
        )

    @pl.loop(1, n_ex)
    def _(k):
        pl.semaphore_signal(
            barrier, inc=1, device_id=(my_dp, lax.rem(my_ex + k, n_ex)), device_id_type=MESH
        )

    def in_copies(k):
        part = pl.ds(k * depth, depth)
        return (
            pltpu.make_async_copy(w_gate.at[0, part, :], wg.at[k], wg_sem.at[k]),
            pltpu.make_async_copy(w_up.at[0, part, :], wu.at[k], wu_sem.at[k]),
        )

    def feature_block(i):
        return lax.rem(my_ex + 1 + i, n_ex)

    def down_copy(i):
        part = pl.ds(pl.multiple_of(feature_block(i) * width, LANES), width)
        return pltpu.make_async_copy(w_down.at[0, :, part], wd.at[i], wd_sem.at[i])

    @pl.loop(0, per_row)
    def _(k):
        for copy in in_copies(k):
            copy.start()

    @pl.loop(0, n_ex)
    def _(i):
        down_copy(i).start()

    row = iota((TILE, n_tok), 0)
    named = jnp.zeros((TILE, n_tok), jnp.int32)
    slot_copies[0].wait()
    for j in range(slots):
        named = jnp.where(row // per_row == j, chosen[0, j, my_ex], named)
    hit = named == iota((TILE, n_tok), 1)
    select = [one_hot(jnp.logical_and(hit, row % per_row == k)) for k in range(per_row)]
    tok_copy.wait()
    for h in range(PARTS):
        picked = jnp.zeros((TILE, half), jnp.float32)
        for k in range(per_row):
            start = (h * per_row + k) * half
            picked += matmul(select[k], tok[:, start:start + half])
        pick[h] = picked.astype(jnp.bfloat16)

    pl.semaphore_wait(barrier, n_dp - 1 + n_ex - 1)

    for h in range(PARTS):
        @pl.loop(1, n_dp)
        def _(k):
            pltpu.make_async_remote_copy(
                src_ref=pick.at[h], dst_ref=gathered.at[h, my_dp],
                send_sem=pick_send, recv_sem=pick_recv.at[h],
                device_id=(lax.rem(my_dp + k, n_dp), my_ex), device_id_type=MESH,
            ).start()

        pltpu.make_async_copy(pick.at[h], gathered.at[h, my_dp], pick_recv.at[h]).start()

    @pl.loop(1, n_ex)
    def _(k):
        pl.semaphore_signal(
            column_sem, inc=1, device_id=(my_dp, lax.rem(my_ex + k, n_ex)), device_id_type=MESH
        )

    gate[...] = jnp.zeros_like(gate)
    up[...] = jnp.zeros_like(up)
    to = iota(back_perm.shape, 0)
    source = iota(back_perm.shape, 1)
    place = to % block
    back_perm[...] = one_hot(
        jnp.logical_and(
            source == (place % pieces) * rows + (to // block) * slots + place // pieces,
            place < slots * pieces,
        )
    )

    weight_rows = n_ex * block
    wrow = iota((weight_rows, LANES), 0)
    wslot = (wrow // block) * slots + (wrow % block) // pieces
    wvalid = wrow % block < slots * pieces
    weight = jnp.zeros((weight_rows, LANES), jnp.float32)
    column = iota((n_tok, weight_rows), 1)
    cslot = (column // block) * slots + (column % block) // pieces
    cvalid = column % block < slots * pieces
    token_of = jnp.full((n_tok, weight_rows), -1, jnp.int32)
    for copy in slot_copies[1:]:
        copy.wait()
    for e in range(n_ex):
        for j in range(slots):
            own = codes[0, j, e].astype(jnp.float32) / 65536.0
            own = jnp.where(j < counts[0, e], own, 0.0)
            weight = jnp.where(jnp.logical_and(wvalid, wslot == e * slots + j), own, weight)
            token_of = jnp.where(
                jnp.logical_and(cvalid, cslot == e * slots + j), chosen[0, j, e], token_of
            )
    scatter = one_hot(token_of == iota((n_tok, weight_rows), 0))

    to = iota((rows, n_dp * TILE), 0)
    source = iota((rows, n_dp * TILE), 1)
    first = (to // slots) * TILE + (to % slots) * per_row
    spread = [one_hot(source == first + k) for k in range(per_row)]
    for h in range(PARTS):
        pltpu.make_async_copy(gathered.at[h], gathered.at[h], pick_recv.at[h]).wait()
        stacked = gathered[h].reshape(n_dp * TILE, half)
        for k in range(per_row):
            q = h * per_row + k
            lhs[q // PARTS, :, (q % PARTS) * half:(q % PARTS + 1) * half] = (
                matmul(spread[k], stacked).astype(jnp.bfloat16)
            )

        @pl.loop(h * per_row // PARTS, (h + 1) * per_row // PARTS)
        def _(k):
            for copy in in_copies(k):
                copy.wait()
            gate[...] += matmul(lhs[k], wg[k])
            up[...] += matmul(lhs[k], wu[k])

    pl.semaphore_wait(column_sem, n_ex - 1)
    value = gate[...]
    hidden[...] = (value / (1.0 + jnp.exp(-value)) * up[...]).astype(jnp.bfloat16)

    @pl.loop(0, n_ex)
    def _(i):
        f = feature_block(i)
        down_copy(i).wait()
        part = matmul(hidden[...], wd[i]).astype(jnp.bfloat16)
        piled = jnp.concatenate(
            [part[:, c * LANES:(c + 1) * LANES] for c in range(pieces)], axis=0
        )
        ready[i] = matmul(back_perm[...], piled).astype(jnp.bfloat16).reshape(n_dp, block, LANES)

        @pl.loop(0, n_dp)
        def _(k):
            s = lax.rem(my_dp + 1 + k, n_dp)
            own = jnp.logical_and(s == my_dp, f == my_ex)

            @pl.when(jnp.logical_not(own))
            def _():
                pltpu.make_async_remote_copy(
                    src_ref=ready.at[i, s], dst_ref=landed.at[me],
                    send_sem=back_send, recv_sem=back_recv,
                    device_id=(s, f), device_id_type=MESH,
                ).start()

            @pl.when(own)
            def _():
                pltpu.make_async_copy(ready.at[i, s], landed.at[me], back_recv).start()

    pltpu.make_async_copy(landed, landed, back_recv).wait()

    def add(s, total):
        held = landed[pl.ds(s * n_ex, n_ex)].astype(jnp.float32)
        return total + held.reshape(weight_rows, LANES)

    total = lax.fori_loop(0, n_dp, add, jnp.zeros((weight_rows, LANES), jnp.float32), unroll=n_dp <= 8)
    total = total * weight
    high = total.astype(jnp.bfloat16)
    rest = total - high.astype(jnp.float32)
    low = rest.astype(jnp.bfloat16)
    spot = (wrow % block) % pieces
    for c in range(pieces):
        mine = spot == c
        result = matmul(scatter, jnp.where(mine, high.astype(jnp.float32), 0.0).astype(jnp.bfloat16))
        result += matmul(scatter, jnp.where(mine, low.astype(jnp.float32), 0.0).astype(jnp.bfloat16))
        out[:, c * LANES:(c + 1) * LANES] = result.astype(out.dtype)

    sent = gathered.at[:, pl.ds(0, n_dp - 1)]
    pltpu.make_async_copy(sent, sent, pick_send).wait()
    sent = landed.at[pl.ds(0, n - 1)]
    pltpu.make_async_copy(sent, sent, back_send).wait()


def on_device(n_dp, n_ex, tokens, w_gate, w_up, w_down, chosen, counts, gate_codes):
    n_tok, d = tokens.shape
    hidden_units = w_gate.shape[2]
    slots = chosen.shape[2]
    rows = n_dp * slots
    per_row = TILE // slots
    depth = d // per_row
    width = d // n_ex
    pieces = width // LANES
    block = -(-slots * pieces // TILE) * TILE
    n = n_dp * n_ex
    bf16, f32 = jnp.bfloat16, jnp.float32
    dma = pltpu.SemaphoreType.DMA
    hbm = pl.BlockSpec(memory_space=pltpu.HBM)
    return pl.pallas_call(
        functools.partial(moe_kernel, n_dp, n_ex),
        out_shape=jax.ShapeDtypeStruct((n_tok, width), bf16),
        in_specs=[hbm] * 7,
        out_specs=pl.BlockSpec(memory_space=pltpu.VMEM),
        scratch_shapes=[
            pltpu.SMEM((1, slots, n_ex), jnp.int32),
            pltpu.SMEM((1, n_ex), jnp.int32),
            pltpu.SMEM((1, slots, n_ex), jnp.int32),
            pltpu.VMEM((n_tok, d), bf16),
            pltpu.VMEM((per_row, depth, hidden_units), bf16),
            pltpu.VMEM((per_row, depth, hidden_units), bf16),
            pltpu.VMEM((n_ex, hidden_units, width), bf16),
            pltpu.VMEM((PARTS, TILE, depth // PARTS), bf16),
            pltpu.VMEM((PARTS, n_dp, TILE, depth // PARTS), bf16),
            pltpu.VMEM((per_row, rows, depth), bf16),
            pltpu.VMEM((rows, hidden_units), f32),
            pltpu.VMEM((rows, hidden_units), f32),
            pltpu.VMEM((rows, hidden_units), bf16),
            pltpu.VMEM((n_dp * block, pieces * rows), bf16),
            pltpu.VMEM((n_ex, n_dp, block, LANES), bf16),
            pltpu.VMEM((n, block, LANES), bf16),
            dma((3,)),
            dma,
            dma((per_row,)),
            dma((per_row,)),
            dma((n_ex,)),
            dma,
            dma((PARTS,)),
            dma,
            dma,
            pltpu.SemaphoreType.REGULAR,
        ],
        compiler_params=pltpu.CompilerParams(
            collective_id=0, has_side_effects=True, vmem_limit_bytes=60 * 1024 * 1024
        ),
        cost_estimate=pl.CostEstimate(
            flops=6 * rows * d * hidden_units,
            bytes_accessed=6 * d * hidden_units,
            transcendentals=rows * hidden_units,
        ),
    )(chosen.transpose(1, 2, 0), counts.T, gate_codes.transpose(1, 2, 0), tokens, w_gate, w_up, w_down)


def solution(mesh):
    placed = (
        P("dp", None),
        P("expert", None, "dp"),
        P("expert", None, "dp"),
        P("expert", "dp", None),
        P(None, "dp", None),
        P(None, "dp"),
        P(None, "dp", None),
    )
    return jax.shard_map(
        functools.partial(on_device, mesh.shape["dp"], mesh.shape["expert"]),
        mesh=mesh, in_specs=placed, out_specs=P("dp", "expert"), check_vma=False,
    )
```
